32 devices in a mesh: col: 16 (over z, y, x), row: 2 (over core).
Axes of the slice: x: 2, y: 2, z: 4, core: 2. Of those that a mesh axis runs over, the one named last changes fastest.
Arguments:
- features: bfloat16 [64, 32768], P(None, ('col', 'row')), may hold values from -6 to 6
- preact: bfloat16 [64, 32768], P(None, ('col', 'row')), may hold values from -8 to 8
- coarse_grad: bfloat16 [128, 4096], P(None, ('col', 'row')), may hold values from -6 to 6
- kernel_one: bfloat16 [27, 64, 64], replicated, may hold values from -0.15625 to 0.15625
- kernel_two: bfloat16 [8, 128, 64], replicated, may hold values from -0.25 to 0.25
- neighbours: int32 [27, 32768], P(None, ('col', 'row')), may hold values from 0 to 3040, as said below
- send_list: int32 [7168], P(('col', 'row')), may hold values from 0 to 1023, as said below
- parent_slot: int32 [32768], P(('col', 'row')), may hold values from 0 to 127, as said below
- child_pos: int32 [32768], P(('col', 'row')), may hold values from 0 to 7, as said below
Outputs:
- feature_grad: bfloat16 [64, 32768], P(None, ('col', 'row'))
- kernel_one_grad: float32 [27, 64, 64], replicated
- kernel_two_grad: float32 [8, 128, 64], replicated
The draws below stay inside these ranges and needn't reach their ends.
Inputs may be any that keep to these rules, and one draw needn't show every extreme that they name: Entries come from the geometry of occupied fine voxels in 16 x 16 x (256) columns, one column a device: neighbour relations are mutual (N(i, o) = j exactly when N(j, 26 - o) = i), entries of 3040 mark empty neighbours, and remote entries only name devices beside the holder along col and row. `send_list`: distinct voxels of the holding device, exactly those that lie on the outermost fine layer of its column along x or y. `parent_slot`: the coarse level is spread over col by a load hash: every value names the parent of exactly 8 fine voxels of the device, so each device along col owns 8 parents of each device of the same row index. `child_pos`: the 8 children of a parent have distinct positions.
All inputs are finite; a program needn't handle non-finite values.
Results may differ from the reference program's by a relative error of at most 0.0049.
Values may be sent and summed in bfloat16 or wider, within the bound.
A program may use at most 64 MiB of HBM per device.

```python
import jax
import jax.numpy as jnp
import numpy as np
from jax import lax

C1 = 64
C2 = 128
PARENTS = 128
QZ = 128
SITES = 1024
BSIDE = 32
BCORN = 16
HCAP = 224
PCAP = 8
SITES_ALL = 32768
N_COL = 16
N_ROW = 2


def layout_tables():
    cells = np.arange(64)
    across = cells // 8
    along = cells % 8
    rim_x = (across == 0) | (across == 7)
    rim_y = (along == 0) | (along == 7)
    corner = rim_x & rim_y
    side = (rim_x | rim_y) & ~corner
    inner = ~(rim_x | rim_y)
    return (cells[side].astype(np.int32), cells[corner].astype(np.int32), cells[inner].astype(np.int32))


def device_plan(dev_key):
    keys = jax.random.split(dev_key, 5)
    side_cells, corner_cells, inner_cells = layout_tables()
    inner_count = PARENTS - BSIDE - BCORN
    side_pick = jax.random.permutation(keys[0], side_cells.shape[0] * QZ)[:BSIDE].astype(jnp.int32)
    corner_pick = jax.random.permutation(keys[1], corner_cells.shape[0] * QZ)[:BCORN].astype(jnp.int32)
    inner_pick = jax.random.permutation(keys[2], inner_cells.shape[0] * QZ)[:inner_count].astype(jnp.int32)
    cell = jnp.concatenate([jnp.asarray(side_cells)[side_pick // QZ], jnp.asarray(corner_cells)[corner_pick // QZ], jnp.asarray(inner_cells)[inner_pick // QZ]])
    height = jnp.concatenate([side_pick % QZ, corner_pick % QZ, inner_pick % QZ])
    slot_ids = jnp.arange(SITES, dtype=jnp.int32)
    slot_cell = cell[slot_ids // 8]
    slot_child = slot_ids % 8
    local_x = 2 * (slot_cell // 8) + slot_child // 4
    local_y = 2 * (slot_cell % 8) + slot_child // 2 % 2
    outer = (local_x == 0) | (local_x == 15) | (local_y == 0) | (local_y == 15)
    rank_key = jnp.where(outer, 0, SITES).astype(jnp.int32) + slot_ids
    slot_perm = jnp.argsort(rank_key, stable=True).astype(jnp.int32)
    shuffled = jax.random.permutation(keys[3], SITES).astype(jnp.int32)
    voxel_of_rank = ((shuffled - shuffled[0] + SITES - 1) % SITES).astype(jnp.int32)
    order = jnp.zeros((SITES,), jnp.int32).at[voxel_of_rank].set(slot_perm)
    rank_of = jnp.zeros((SITES,), jnp.int32).at[voxel_of_rank].set(slot_ids)
    owner_slot = jax.random.permutation(keys[4], PARENTS).astype(jnp.int32)
    return (cell, height, order, rank_of, voxel_of_rank[:HCAP], owner_slot)


def world_plan(key):
    base = jax.random.fold_in(key, 7301)
    devices = N_COL * N_ROW
    cell, height, order, rank_of, offered, owner_slot = jax.vmap(device_plan)(jax.random.split(base, devices))
    parent = order // 8
    child = order % 8
    dev_ids = jnp.arange(devices, dtype=jnp.int32)[:, None]
    pcell = jnp.take_along_axis(cell, parent, axis=1)
    pheight = jnp.take_along_axis(height, parent, axis=1)
    fine_x = dev_ids // N_ROW * 16 + 2 * (pcell // 8) + child // 4
    fine_y = dev_ids % N_ROW * 16 + 2 * (pcell % 8) + child // 2 % 2
    fine_z = 2 * pheight + child % 2
    size_x = 16 * N_COL
    size_y = 16 * N_ROW
    size_z = 2 * QZ
    ident = dev_ids * SITES + jnp.arange(SITES, dtype=jnp.int32)[None, :]
    grid = jnp.full((size_x, size_y, size_z), -1, jnp.int32).at[fine_x, fine_y, fine_z].set(ident)
    flat_rank = rank_of.reshape(-1)
    sentinel = SITES + 9 * HCAP
    rows_out = []
    for step_x in (-1, 0, 1):
        for step_y in (-1, 0, 1):
            for step_z in (-1, 0, 1):
                near_x = fine_x + step_x
                near_y = fine_y + step_y
                near_z = fine_z + step_z
                inside = (near_x >= 0) & (near_x < size_x) & (near_y >= 0) & (near_y < size_y) & (near_z >= 0) & (near_z < size_z)
                found = grid[jnp.clip(near_x, 0, size_x - 1), jnp.clip(near_y, 0, size_y - 1), jnp.clip(near_z, 0, size_z - 1)]
                found = jnp.where(inside, found, -1)
                safe = jnp.maximum(found, 0)
                near_dev = safe // SITES
                near_site = safe % SITES
                move_col = near_dev // N_ROW - dev_ids // N_ROW
                move_row = near_dev % N_ROW - dev_ids % N_ROW
                remote = SITES + ((move_col + 1) * 3 + move_row + 1) * HCAP + flat_rank[safe]
                entry = jnp.where(found < 0, sentinel, jnp.where(near_dev == dev_ids, near_site, remote))
                rows_out.append(entry.reshape(-1).astype(jnp.int32))
    neighbours = jnp.stack(rows_out)
    send = offered.reshape(-1).astype(jnp.int32)
    slots = jnp.take_along_axis(owner_slot, parent, axis=1).reshape(-1)
    return (neighbours, send, slots, child.reshape(-1).astype(jnp.int32))


def draw_neighbours(key, part):
    return world_plan(key)[0]


def draw_send_list(key, part):
    return world_plan(key)[1]


def draw_parent_slot(key, part):
    return world_plan(key)[2]


def draw_child_pos(key, part):
    return world_plan(key)[3]


def level_of(rng, dims, cuts, least, high):
    def one(axis_at, shards_of):
        steps = jax.random.uniform(jax.random.fold_in(jax.random.fold_in(rng, 6), axis_at), (shards_of,), jnp.float32, least / len(cuts), high / len(cuts))
        return jnp.repeat(jnp.exp(steps), dims[axis_at] // shards_of).reshape((-1,) + (1,) * (len(dims) - axis_at - 1))

    gain = one(*cuts[0])
    for cut in cuts[1:]:
        gain = gain * one(*cut)
    return gain


def noise(stream_key, shape, deviation, limit, cuts=(), held_as=jnp.bfloat16):
    values = jax.random.normal(stream_key, shape, jnp.float32) * deviation
    if len(cuts) > 0:
        values = level_of(stream_key, shape, cuts, -0.22, 0.18) * values
    return jnp.clip(values, min=-limit, max=limit).astype(held_as)


def setup_inputs(seed: int = 0) -> dict:
    arg_keys = jax.random.split(jax.random.key(seed), 10)
    return {
        "features": noise(arg_keys[0], (C1, SITES_ALL), 1.0, 6.0, ((1, 32),)),
        "preact": noise(arg_keys[1], (C1, SITES_ALL), 1.5, 8.0, ((1, 32),)),
        "coarse_grad": noise(arg_keys[2], (C2, PARENTS * N_COL * N_ROW), 1.0, 6.0, ((1, 32),)),
        "kernel_one": noise(arg_keys[3], (27, C1, C1), (27 * C1) ** -0.5, 0.15625),
        "kernel_two": noise(arg_keys[4], (8, C2, C1), (8 * C1) ** -0.5, 0.25),
        "neighbours": draw_neighbours(jax.random.fold_in(arg_keys[9], 71), 0),
        "send_list": draw_send_list(jax.random.fold_in(arg_keys[9], 71), 0),
        "parent_slot": draw_parent_slot(jax.random.fold_in(arg_keys[9], 71), 0),
        "child_pos": draw_child_pos(jax.random.fold_in(arg_keys[9], 71), 0),
    }


def reference(features, preact, coarse_grad, kernel_one, kernel_two, neighbours, send_list, parent_slot, child_pos):
    all_sites = SITES * N_COL * N_ROW
    device = jnp.arange(all_sites, dtype=jnp.int32) // SITES
    dev_col = device // N_ROW
    dev_row = device % N_ROW
    owner = parent_slot // PCAP
    spot = parent_slot % PCAP
    coarse_index = ((owner * N_ROW + dev_row) * PARENTS + dev_col * PCAP + spot).astype(jnp.int32)
    parent_grad = jnp.take(coarse_grad, coarse_index, axis=1)
    pre = preact.astype(jnp.float32)
    gate_sig = jax.nn.sigmoid(pre)
    act = (pre * gate_sig).astype(jnp.bfloat16)

    def per_child(carry, pieces):
        weight, which = pieces
        picked = child_pos == which
        product = jnp.dot(weight.T, parent_grad, preferred_element_type=jnp.float32)
        carry = carry + jnp.where(picked[None, :], product, 0.0)
        masked = jnp.where(picked[None, :], act, jnp.zeros_like(act))
        grad_w = jnp.dot(parent_grad, masked.T, preferred_element_type=jnp.float32)
        return carry, grad_w

    act_grad, two_sum = lax.scan(per_child, jnp.zeros((C1, all_sites), jnp.float32),
                                 (kernel_two, jnp.arange(8, dtype=jnp.int32)))
    pre_grad = (act_grad * gate_sig * (1.0 + pre * (1.0 - gate_sig))).astype(jnp.bfloat16)

    rel = neighbours - SITES
    group = jnp.clip(rel // HCAP, 0, 8)
    place = jnp.clip(rel % HCAP, 0, HCAP - 1)
    near_col = jnp.clip(dev_col[None, :] + group // 3 - 1, 0, N_COL - 1)
    near_row = jnp.clip(dev_row[None, :] + group % 3 - 1, 0, N_ROW - 1)
    other = near_col * N_ROW + near_row
    remote = other * SITES + jnp.take(send_list, other * HCAP + place)
    local = device[None, :] * SITES + neighbours
    glob = jnp.where(neighbours < SITES, local,
                     jnp.where(neighbours < SITES + 9 * HCAP, remote, all_sites)).astype(jnp.int32)
    feat_table = jnp.concatenate([features, jnp.zeros((C1, 1), jnp.bfloat16)], axis=1)
    grad_table = jnp.concatenate([pre_grad, jnp.zeros((C1, 1), jnp.bfloat16)], axis=1)

    def per_offset(carry, pieces):
        near, mirror, weight = pieces
        near_feat = jnp.take(feat_table, near, axis=1)
        grad_w = jnp.dot(pre_grad, near_feat.T, preferred_element_type=jnp.float32)
        near_grad = jnp.take(grad_table, mirror, axis=1)
        carry = carry + jnp.dot(weight.T, near_grad, preferred_element_type=jnp.float32)
        return carry, grad_w

    feat_grad, one_sum = lax.scan(per_offset, jnp.zeros((C1, all_sites), jnp.float32),
                                  (glob, glob[::-1], kernel_one))
    scale = float(all_sites) ** -0.5
    return feat_grad.astype(jnp.bfloat16), one_sum * scale, two_sum * scale
```

```python
import functools

import jax
import jax.numpy as jnp
from jax import lax
from jax.experimental import pallas as pl
from jax.experimental.pallas import tpu as pltpu
from jax.sharding import PartitionSpec as P

F32 = jnp.float32
BF16 = jnp.bfloat16
NT = (((1,), (1,)), ((), ()))
TN = (((0,), (0,)), ((), ()))
MESH = pl.DeviceIdType.MESH
BESIDE = [(x, y) for x in (-1, 0, 1) for y in (-1, 0, 1) if (x, y) != (0, 0)]


def pick(index_row, rows):
    n = index_row.shape[1]
    spot = lax.broadcasted_iota(jnp.int32, (rows, n), 0)
    return jnp.where(spot == index_row, 1.0, 0.0).astype(BF16)


def dot(a, b, dims=(((1,), (0,)), ((), ()))):
    return lax.dot_general(a, b, dims, preferred_element_type=F32)


def remote(src, dst, send_sem, recv_sem, col, row):
    return pltpu.make_async_remote_copy(
        src_ref=src, dst_ref=dst, send_sem=send_sem, recv_sem=recv_sem,
        device_id=(col, row), device_id_type=MESH)


def others(me, count, step):
    def one(j, carry):
        step(lax.rem(me + j, count))
        return carry
    lax.fori_loop(1, count, one, 0)


def kernel(sizes, coarse_ref, slot_ref, child_ref, preact_ref, feat_ref, two_ref, one_ref, nb_ref,
           send_ref, feat_out_ref, sum_ref,
           owners, grad, offer, halo, ng, ngr, feat_two, part, row_in, mid, col_in, fin,
           coarse_sems, halo_sems, row_sems, col_sems, gather_col_sems, gather_row_sems):
    n_col, n_row, width, held, share = sizes
    channels, sites = feat_ref.shape
    offsets = nb_ref.shape[0]
    pairs = (offsets + 1) // 2
    padded = send_ref.shape[1]
    tile = 256
    c, r = lax.axis_index("col"), lax.axis_index("row")

    def beside(x, y):
        return ((c + x >= 0) & (c + x < n_col) & (r + y >= 0) & (r + y < n_row))

    barrier = pltpu.get_barrier_semaphore()

    def greet(col, row):
        pl.semaphore_signal(barrier, inc=1, device_id=(col, row), device_id_type=MESH)

    others(c, n_col, lambda peer: greet(peer, r))
    others(r, n_row, lambda peer: greet(c, peer))
    count = n_col - 1 + n_row - 1
    for x, y in BESIDE:
        if x != 0 and y != 0:
            there = beside(x, y)

            @pl.when(there)
            def _():
                greet(c + x, r + y)

            count = count + jnp.where(there, 1, 0)
    pl.semaphore_wait(barrier, count)

    def coarse_copy(src_col, dst_col, to):
        return remote(coarse_ref.at[dst_col], owners.at[src_col], coarse_sems.at[0, dst_col],
                      coarse_sems.at[1, src_col], to, r)

    others(c, n_col, lambda peer: coarse_copy(c, peer, peer).start())
    owners[pl.ds(c, 1)] = coarse_ref[pl.ds(c, 1)]
    pre = preact_ref[...].astype(F32)
    gate = jax.nn.sigmoid(pre)
    act = (pre * gate).astype(BF16).astype(F32)
    slot = slot_ref[...]
    lines = owners.shape[1]
    line = slot // held * lines + slot % held
    chosen_parent = pick(line, n_col * lines)
    child = child_ref[...]
    for x, y in BESIDE:
        @pl.when(jnp.logical_not(beside(x, y)))
        def _():
            halo[(x + 1) * 3 + y + 1] = jnp.zeros(halo.shape[1:], BF16)
    ng[pl.ds(offsets * channels, channels), :] = jnp.zeros((channels, sites), BF16)
    ngr[pl.ds(offsets * channels, channels), :] = jnp.zeros((channels, padded), BF16)
    feat_two[0, pl.ds(0, channels), :] = feat_ref[...]
    feat_two[0, pl.ds(channels, channels), :] = jnp.zeros((channels, sites), BF16)
    feat_two[1, pl.ds(0, channels), :] = jnp.zeros((channels, sites), BF16)
    feat_two[1, pl.ds(channels, channels), :] = feat_ref[...]
    others(c, n_col, lambda peer: coarse_copy(peer, c, c).wait_recv())
    all_owned = owners[...].reshape(n_col * lines, owners.shape[2])
    parent = dot(all_owned.astype(F32).T.astype(BF16), chosen_parent).astype(BF16)
    act_grad = jnp.zeros((channels, sites), F32)
    for k in range(8):
        rows = pl.ds(k * channels, channels)
        here = jnp.broadcast_to(child == k, (channels, sites))
        act_grad = jnp.where(here, dot(two_ref[rows, :], parent), act_grad)
    grad[...] = (act_grad * gate * (1.0 + pre * (1.0 - gate))).astype(BF16)
    chosen = pick(send_ref[...], sites)
    offer[...] = dot(grad[...], chosen).astype(BF16)

    def halo_copy(x, y):
        b = (x + 1) * 3 + y + 1
        return remote(offer, halo.at[8 - b], halo_sems.at[0, b], halo_sems.at[1, 8 - b],
                      c + x, r + y)

    for x, y in BESIDE:
        @pl.when(beside(x, y))
        def _():
            halo_copy(x, y).start()

    base = pairs * channels
    for k in range(8):
        here = jnp.broadcast_to(child == k, (channels, sites))
        masked = jnp.where(here, act, 0.0).astype(BF16)
        part[pl.ds(base + k * channels, channels), :] = dot(masked, parent, NT).astype(BF16)
    spare = base + 8 * channels
    if part.shape[0] > spare:
        part[pl.ds(spare, part.shape[0] - spare), :] = jnp.zeros(
            (part.shape[0] - spare, part.shape[1]), BF16)

    def near(o, carry):
        rows = pl.ds(pl.multiple_of(o * channels, channels), channels)
        for at in range(0, sites, tile):
            columns = pl.ds(at, tile)
            ng[rows, columns] = dot(
                grad[...], pick(nb_ref[pl.ds(offsets - 1 - o, 1), columns], sites)
            ).astype(BF16)
        return carry

    lax.fori_loop(0, offsets, near, 0)
    feat_grad = dot(one_ref[...], ng[...], TN)
    one_grad = dot(ng[pl.ds(0, base), :], feat_two[0], NT) + dot(
        ng[pl.ds(base, base), :], feat_two[1], NT)

    nb = nb_ref[...]
    high = nb // 64
    low = nb - high * 64
    rim_high = dot(high.astype(F32).astype(BF16), chosen)
    rim_low = dot(low.astype(F32).astype(BF16), chosen)
    rim = (rim_high * 64.0 + rim_low).astype(jnp.int32)
    rim_feat = [dot(feat_two[i], chosen).astype(BF16) for i in range(2)]
    for x, y in BESIDE:
        @pl.when(beside(x, y))
        def _():
            halo_copy(-x, -y).wait_recv()
    for o in range(offsets):
        mirror = offsets - 1 - o
        ex, ey = mirror // 9 - 1, mirror // 3 % 3 - 1
        total = jnp.zeros((channels, padded), F32)
        for gx, gy in sorted({(ex, 0), (0, ey), (ex, ey)} - {(0, 0)}):
            b = (gx + 1) * 3 + gy + 1
            index = rim[mirror:mirror + 1, :] - (sites + b * width)
            total = total + dot(halo[b], pick(index, padded))
        ngr[pl.ds(o * channels, channels), :] = total.astype(BF16)
    extra = dot(one_ref[...], ngr[...], TN)
    head = extra.astype(BF16)
    tail = (extra - head.astype(F32)).astype(BF16)
    feat_out_ref[...] = (feat_grad + dot(head, chosen, NT) + dot(tail, chosen, NT)).astype(BF16)
    one_grad = one_grad + dot(ngr[pl.ds(0, base), :], rim_feat[0], NT) + dot(
        ngr[pl.ds(base, base), :], rim_feat[1], NT)
    part[pl.ds(0, base), :] = one_grad.astype(BF16)

    band = n_col * share

    def row_copy(src_row, dst_row, to):
        return remote(part.at[pl.ds(pl.multiple_of(dst_row * band, band), band)], row_in.at[src_row],
                      row_sems.at[0, dst_row], row_sems.at[1, src_row], c, to)

    others(r, n_row, lambda peer: row_copy(r, peer, peer).start())
    row_in[pl.ds(r, 1)] = part[pl.ds(pl.multiple_of(r * band, band), band), :][None]
    others(r, n_row, lambda peer: row_copy(peer, r, r).wait_recv())
    total = row_in[0].astype(F32)
    for i in range(1, n_row):
        total = total + row_in[i].astype(F32)
    mid[...] = total.astype(BF16)

    def col_copy(src_col, dst_col, to):
        return remote(mid.at[pl.ds(pl.multiple_of(dst_col * share, share), share)],
                      col_in.at[src_col], col_sems.at[0, dst_col], col_sems.at[1, src_col], to, r)

    others(c, n_col, lambda peer: col_copy(c, peer, peer).start())
    col_in[pl.ds(c, 1)] = mid[pl.ds(pl.multiple_of(c * share, share), share), :][None]
    others(c, n_col, lambda peer: col_copy(peer, c, c).wait_recv())
    total = col_in[0].astype(F32)
    for i in range(1, n_col):
        total = total + col_in[i].astype(F32)
    fin[...] = total.astype(BF16)

    def gather_col_copy(src_col, dst_col, to):
        return remote(fin, sum_ref.at[r, src_col], gather_col_sems.at[0, dst_col],
                      gather_col_sems.at[1, src_col], to, r)

    others(c, n_col, lambda peer: gather_col_copy(c, peer, peer).start())
    sum_ref[pl.ds(r, 1), pl.ds(c, 1)] = fin[...][None, None]
    others(c, n_col, lambda peer: gather_col_copy(peer, c, c).wait_recv())

    def gather_row_copy(src_row, dst_row, to):
        return remote(sum_ref.at[src_row], sum_ref.at[src_row], gather_row_sems.at[0, dst_row],
                      gather_row_sems.at[1, src_row], c, to)

    others(r, n_row, lambda peer: gather_row_copy(r, peer, peer).start())
    others(r, n_row, lambda peer: gather_row_copy(peer, r, r).wait_recv())

    others(c, n_col, lambda peer: coarse_copy(c, peer, peer).wait_send())
    for x, y in BESIDE:
        @pl.when(beside(x, y))
        def _():
            halo_copy(x, y).wait_send()
    others(r, n_row, lambda peer: row_copy(r, peer, peer).wait_send())
    others(c, n_col, lambda peer: col_copy(c, peer, peer).wait_send())
    others(c, n_col, lambda peer: gather_col_copy(c, peer, peer).wait_send())
    others(r, n_row, lambda peer: gather_row_copy(r, peer, peer).wait_send())


def body(features, preact, coarse_grad, kernel_one, kernel_two, neighbours, send_list,
         parent_slot, child_pos):
    channels, sites = features.shape
    wide, parents = coarse_grad.shape
    offsets = neighbours.shape[0]
    width = send_list.shape[0]
    padded = -(-width // 128) * 128
    n_col, n_row = lax.axis_size("col"), lax.axis_size("row")
    held = parents // n_col
    lines = -(-held // 16) * 16
    pairs = (offsets + 1) // 2
    rows = (pairs + 8) * channels
    share = -(-rows // (n_col * n_row * 16)) * 16
    shape = jax.ShapeDtypeStruct
    coarse = jnp.pad(coarse_grad.T.reshape(n_col, held, wide), ((0, 0), (0, lines - held), (0, 0)))
    two = kernel_two.transpose(0, 2, 1).reshape(8 * channels, wide)
    one = jnp.pad(kernel_one.reshape(offsets * channels, channels), ((0, channels), (0, 0)))
    send = jnp.pad(send_list, (0, padded - width), constant_values=-1)[None, :]
    args = (coarse, parent_slot[None, :], child_pos[None, :], preact, features, two, one, neighbours,
            send)
    vmem = pl.BlockSpec(memory_space=pltpu.VMEM)
    total = n_row * n_col * share
    feat_grad, sums = pl.pallas_call(
        functools.partial(kernel, (n_col, n_row, width, held, share)),
        out_shape=(shape((channels, sites), BF16), shape((n_row, n_col, share, wide), BF16)),
        in_specs=[vmem] * len(args),
        out_specs=(vmem, vmem),
        scratch_shapes=[
            pltpu.VMEM((n_col, lines, wide), BF16),
            pltpu.VMEM((channels, sites), BF16),
            pltpu.VMEM((channels, padded), BF16),
            pltpu.VMEM((9, channels, padded), BF16),
            pltpu.VMEM((2 * pairs * channels, sites), BF16),
            pltpu.VMEM((2 * pairs * channels, padded), BF16),
            pltpu.VMEM((2, 2 * channels, sites), BF16),
            pltpu.VMEM((total, wide), BF16),
            pltpu.VMEM((n_row, n_col * share, wide), BF16),
            pltpu.VMEM((n_col * share, wide), BF16),
            pltpu.VMEM((n_col, share, wide), BF16),
            pltpu.VMEM((share, wide), BF16),
            pltpu.SemaphoreType.DMA((2, n_col)),
            pltpu.SemaphoreType.DMA((2, 9)),
            pltpu.SemaphoreType.DMA((2, n_row)),
            pltpu.SemaphoreType.DMA((2, n_col)),
            pltpu.SemaphoreType.DMA((2, n_col)),
            pltpu.SemaphoreType.DMA((2, n_row)),
        ],
        compiler_params=pltpu.CompilerParams(
            collective_id=0, has_side_effects=True, vmem_limit_bytes=48 * 1024 * 1024),
    )(*args)
    scale = float(sites * n_col * n_row) ** (-0.5)
    sums = sums.reshape(total, wide).astype(F32) * scale
    one_sum = sums[:pairs * channels].reshape(pairs, channels, wide)
    one_sum = jnp.concatenate([one_sum[:, :, :channels], one_sum[:, :, channels:]])[:offsets]
    two_sum = sums[pairs * channels:rows].reshape(8, channels, wide).transpose(0, 2, 1)
    return feat_grad, one_sum, two_sum


def solution(mesh):
    both = ("col", "row")
    placed = (P(None, both), P(None, both), P(None, both), P(), P(), P(None, both), P(both),
              P(both), P(both))
    return jax.shard_map(body, mesh=mesh, in_specs=placed, out_specs=(P(None, both), P(), P()),
                         check_vma=False)
```

```python
import functools

import jax
import jax.numpy as jnp
from jax import lax
from jax.experimental import pallas as pl
from jax.experimental.pallas import tpu as pltpu
from jax.sharding import PartitionSpec as P

F32 = jnp.float32
BF16 = jnp.bfloat16
NN = (((1,), (0,)), ((), ()))
NT = (((1,), (1,)), ((), ()))
TN = (((0,), (0,)), ((), ()))
MESH = pl.DeviceIdType.MESH
BESIDE = [(x, y) for x in (-1, 0, 1) for y in (-1, 0, 1) if (x, y) != (0, 0)]


def pick(index_row, rows):
    n = index_row.shape[1]
    spot = lax.broadcasted_iota(jnp.int32, (rows, n), 0)
    return jnp.where(spot == index_row, 1.0, 0.0).astype(BF16)


def dot(a, b, dims=NN):
    return lax.dot_general(a, b, dims, preferred_element_type=F32)


def remote(src, dst, send_sem, recv_sem, col, row):
    return pltpu.make_async_remote_copy(
        src_ref=src, dst_ref=dst, send_sem=send_sem, recv_sem=recv_sem,
        device_id=(col, row), device_id_type=MESH)


def others(me, count, step):
    def one(j, carry):
        step(lax.rem(me + j, count))
        return carry
    lax.fori_loop(1, count, one, 0)


class Sum:
    def __init__(self, place, share, part, row_in, mid, col_in, fin, out, row_sems, col_sems,
                 back_col_sems, back_row_sems):
        self.c, self.r, self.n_col, self.n_row = place
        self.share, self.band = share, share * self.n_col
        self.part, self.row_in, self.mid, self.col_in = part, row_in, mid, col_in
        self.fin, self.out = fin, out
        self.sems = (row_sems, col_sems, back_col_sems, back_row_sems)

    def rows(self, step):
        others(self.r, self.n_row, step)

    def cols(self, step):
        others(self.c, self.n_col, step)

    def row_copy(self, src, dst, to):
        cut = pl.ds(pl.multiple_of(dst * self.band, self.band), self.band)
        return remote(self.part.at[cut], self.row_in.at[src], self.sems[0].at[0, dst],
                      self.sems[0].at[1, src], self.c, to)

    def col_copy(self, src, dst, to):
        cut = pl.ds(pl.multiple_of(dst * self.share, self.share), self.share)
        return remote(self.mid.at[cut], self.col_in.at[src], self.sems[1].at[0, dst],
                      self.sems[1].at[1, src], to, self.r)

    def back_col_copy(self, src, dst, to):
        return remote(self.fin, self.out.at[self.r, src], self.sems[2].at[0, dst],
                      self.sems[2].at[1, src], to, self.r)

    def back_row_copy(self, src, dst, to):
        return remote(self.out.at[src], self.out.at[src], self.sems[3].at[0, dst],
                      self.sems[3].at[1, src], self.c, to)

    def start(self):
        self.rows(lambda peer: self.row_copy(self.r, peer, peer).start())
        self.row_in[pl.ds(self.r, 1)] = self.part[
            pl.ds(pl.multiple_of(self.r * self.band, self.band), self.band), :][None]

    def along_col(self):
        self.rows(lambda peer: self.row_copy(peer, self.r, self.r).wait_recv())
        total = self.row_in[0].astype(F32)
        for i in range(1, self.n_row):
            total = total + self.row_in[i].astype(F32)
        self.mid[...] = total.astype(BF16)
        self.cols(lambda peer: self.col_copy(self.c, peer, peer).start())
        self.col_in[pl.ds(self.c, 1)] = self.mid[
            pl.ds(pl.multiple_of(self.c * self.share, self.share), self.share), :][None]

    def back_col(self):
        self.cols(lambda peer: self.col_copy(peer, self.c, self.c).wait_recv())
        total = self.col_in[0].astype(F32)
        for i in range(1, self.n_col):
            total = total + self.col_in[i].astype(F32)
        self.fin[...] = total.astype(BF16)
        self.cols(lambda peer: self.back_col_copy(self.c, peer, peer).start())
        self.out[pl.ds(self.r, 1), pl.ds(self.c, 1)] = self.fin[...][None, None]

    def back_row(self):
        self.cols(lambda peer: self.back_col_copy(peer, self.c, self.c).wait_recv())
        self.rows(lambda peer: self.back_row_copy(self.r, peer, peer).start())

    def end(self):
        self.rows(lambda peer: self.back_row_copy(peer, self.r, self.r).wait_recv())
        self.rows(lambda peer: self.row_copy(self.r, peer, peer).wait_send())
        self.cols(lambda peer: self.col_copy(self.c, peer, peer).wait_send())
        self.cols(lambda peer: self.back_col_copy(self.c, peer, peer).wait_send())
        self.rows(lambda peer: self.back_row_copy(self.r, peer, peer).wait_send())


def offset_of(x, y, z):
    return (x + 1) * 9 + (y + 1) * 3 + z + 1


def bits(child):
    return child // 4, child // 2 % 2, child % 2


def kernel(sizes, coarse_ref, slot_ref, child_ref, preact_ref, feat_ref, two_ref, one_ref, nb_ref,
           send_ref, feat_out_ref, one_sum_ref, two_sum_ref,
           owners, grad, offer, halo, ng, ngr, feat_two, sort, moves, *rest):
    n_col, n_row, width, held, one_share, two_share = sizes
    channels, sites = feat_ref.shape
    parents = sites // 8
    offsets = nb_ref.shape[0]
    pairs = (offsets + 1) // 2
    padded = send_ref.shape[1]
    c, r = lax.axis_index("col"), lax.axis_index("row")
    place = (c, r, n_col, n_row)
    one_sum = Sum(place, one_share, *rest[0:5], one_sum_ref, *rest[10:14])
    two_sum = Sum(place, two_share, *rest[5:10], two_sum_ref, *rest[14:18])
    coarse_sems, halo_sems = rest[18:]

    def beside(x, y):
        return ((c + x >= 0) & (c + x < n_col) & (r + y >= 0) & (r + y < n_row))

    barrier = pltpu.get_barrier_semaphore()

    def greet(col, row):
        pl.semaphore_signal(barrier, inc=1, device_id=(col, row), device_id_type=MESH)

    others(c, n_col, lambda peer: greet(peer, r))
    others(r, n_row, lambda peer: greet(c, peer))
    count = n_col - 1 + n_row - 1
    for x, y in BESIDE:
        if x != 0 and y != 0:
            there = beside(x, y)

            @pl.when(there)
            def _():
                greet(c + x, r + y)

            count = count + jnp.where(there, 1, 0)
    pl.semaphore_wait(barrier, count)

    def coarse_copy(src_col, dst_col, to):
        return remote(coarse_ref.at[dst_col], owners.at[src_col], coarse_sems.at[0, dst_col],
                      coarse_sems.at[1, src_col], to, r)

    others(c, n_col, lambda peer: coarse_copy(c, peer, peer).start())
    owners[pl.ds(c, 1)] = coarse_ref[pl.ds(c, 1)]
    for x, y in BESIDE:
        @pl.when(jnp.logical_not(beside(x, y)))
        def _():
            halo[(x + 1) * 3 + y + 1] = jnp.zeros(halo.shape[1:], BF16)

    nb = nb_ref[...]
    high = nb // 64
    low = (nb - high * 64).astype(F32).astype(BF16)
    high = high.astype(F32).astype(BF16)

    def entries(onehot, dims=NN):
        return (dot(high, onehot, dims) * 64.0 + dot(low, onehot, dims)).astype(jnp.int32)

    slot = slot_ref[...]
    child = child_ref[...]
    kinds = lax.broadcasted_iota(jnp.int32, (128, sites), 0)
    first = jnp.where((kinds == child) & (slot == 0), 1.0, 0.0).astype(BF16)
    first_nb = entries(first, NT)
    slot_mark = jnp.broadcast_to((slot + 1).astype(F32), (16, sites)).astype(BF16)
    kind = jnp.zeros((16, 128), F32)
    for weight, o in ((4.0, offset_of(-1, 0, 0)), (2.0, offset_of(0, -1, 0)),
                      (1.0, offset_of(0, 0, -1))):
        mark = dot(slot_mark, pick(first_nb[o:o + 1, :], sites))
        kind = kind + jnp.where(mark == 1.0, weight, 0.0)
    corner = dot(kind.astype(BF16), pick(child, 128))[0:1, :].astype(jnp.int32)

    sort[...] = pick(corner * parents + slot, sites)
    feat = dot(feat_ref[...], sort[...], NT).astype(BF16)
    feat_two[0, pl.ds(0, channels), :] = feat
    feat_two[0, pl.ds(channels, channels), :] = jnp.zeros((channels, sites), BF16)
    feat_two[1, pl.ds(0, channels), :] = jnp.zeros((channels, sites), BF16)
    feat_two[1, pl.ds(channels, channels), :] = feat
    sorted_nb = entries(sort[...], NT)
    chosen_slot = pick(slot, parents)
    for o in range(offsets):
        if o != offsets // 2:
            x, y, z = o // 9 - 1, o // 3 % 3 - 1, o % 3 - 1
            at = ((x > 0) * 4 + (y > 0) * 2 + (z > 0)) * parents
            moves[o] = dot(
                chosen_slot, pick(sorted_nb[o:o + 1, at:at + parents], sites)).astype(BF16)
    chosen = pick(send_ref[...], sites)
    rim = entries(chosen)
    rim_feat = dot(feat_ref[...], chosen).astype(BF16)
    blank = jnp.zeros(rim_feat.shape, BF16)

    pre = preact_ref[...].astype(F32)
    gate = jax.nn.sigmoid(pre)
    act = (pre * gate).astype(BF16).astype(F32)
    lines = owners.shape[1]
    chosen_parent = pick(slot // held * lines + slot % held, n_col * lines)
    ng[pl.ds(offsets * channels, channels), :] = jnp.zeros((channels, sites), BF16)
    ngr[pl.ds(offsets * channels, channels), :] = jnp.zeros((channels, padded), BF16)
    others(c, n_col, lambda peer: coarse_copy(peer, c, c).wait_recv())
    all_owned = owners[...].reshape(n_col * lines, owners.shape[2])
    parent = dot(all_owned.astype(F32).T.astype(BF16), chosen_parent).astype(BF16)
    act_grad = jnp.zeros((channels, sites), F32)
    for k in range(8):
        rows = pl.ds(k * channels, channels)
        here = jnp.broadcast_to(child == k, (channels, sites))
        act_grad = jnp.where(here, dot(two_ref[rows, :], parent), act_grad)
    grad[...] = (act_grad * gate * (1.0 + pre * (1.0 - gate))).astype(BF16)
    offer[...] = dot(grad[...], chosen).astype(BF16)

    def halo_copy(x, y):
        b = (x + 1) * 3 + y + 1
        return remote(offer, halo.at[8 - b], halo_sems.at[0, b], halo_sems.at[1, 8 - b],
                      c + x, r + y)

    for x, y in BESIDE:
        @pl.when(beside(x, y))
        def _():
            halo_copy(x, y).start()

    two_rows = 8 * channels
    for k in range(8):
        here = jnp.broadcast_to(child == k, (channels, sites))
        masked = jnp.where(here, act, 0.0).astype(BF16)
        two_sum.part[pl.ds(k * channels, channels), :] = dot(masked, parent, NT).astype(BF16)
    base = pairs * channels
    for piece, used in ((two_sum.part, two_rows), (one_sum.part, base)):
        spare = piece.shape[0] - used
        if spare > 0:
            piece[pl.ds(used, spare), :] = jnp.zeros((spare, piece.shape[1]), BF16)
    two_sum.start()

    near = dot(grad[...], sort[...], NT).astype(BF16)
    blocks = [near[:, k * parents:(k + 1) * parents] for k in range(8)]
    found = {((0, 0, 0), k): blocks[k] for k in range(8)}
    for o in range(offsets):
        if o != offsets // 2:
            step = (o // 9 - 1, o // 3 % 3 - 1, o % 3 - 1)
            ends = [k for k in range(8)
                    if all(s == 0 or b == (s < 0) for s, b in zip(step, bits(k)))]
            moved = dot(jnp.concatenate([blocks[k] for k in ends], axis=0), moves[o]).astype(BF16)
            for i, k in enumerate(ends):
                found[step, k] = moved[i * channels:(i + 1) * channels, :]
    for o in range(offsets):
        move = (1 - o // 9, 1 - o // 3 % 3, 1 - o % 3)
        for k in range(8):
            to = [b + m for b, m in zip(bits(k), move)]
            end = to[0] % 2 * 4 + to[1] % 2 * 2 + to[2] % 2
            ng[pl.ds(o * channels, channels), pl.ds(k * parents, parents)] = (
                found[tuple(t // 2 for t in to), end])
    two_sum.along_col()
    spread = dot(one_ref[...], ng[pl.ds(0, offsets * channels), :], TN)

    def split(values):
        head = values.astype(BF16)
        return head, (values - head.astype(F32)).astype(BF16)

    head, tail = split(spread)
    feat_grad = dot(head, sort[...]) + dot(tail, sort[...])
    one_grad = dot(ng[pl.ds(0, base), :], feat_two[0], NT) + dot(
        ng[pl.ds(base, base), :], feat_two[1], NT)

    for x, y in BESIDE:
        @pl.when(beside(x, y))
        def _():
            halo_copy(-x, -y).wait_recv()
    for o in range(offsets):
        mirror = offsets - 1 - o
        ex, ey = mirror // 9 - 1, mirror // 3 % 3 - 1
        total = jnp.zeros((channels, padded), F32)
        for gx, gy in sorted({(ex, 0), (0, ey), (ex, ey)} - {(0, 0)}):
            b = (gx + 1) * 3 + gy + 1
            index = rim[mirror:mirror + 1, :] - (sites + b * width)
            total = total + dot(halo[b], pick(index, padded))
        ngr[pl.ds(o * channels, channels), :] = total.astype(BF16)
    one_grad = one_grad + dot(
        ngr[pl.ds(0, base), :], jnp.concatenate([rim_feat, blank], axis=0), NT) + dot(
        ngr[pl.ds(base, base), :], jnp.concatenate([blank, rim_feat], axis=0), NT)
    one_sum.part[pl.ds(0, base), :] = one_grad.astype(BF16)
    one_sum.start()
    two_sum.back_col()
    one_sum.along_col()
    head, tail = split(dot(one_ref[...], ngr[pl.ds(0, offsets * channels), :], TN))
    feat_out_ref[...] = (feat_grad + dot(head, chosen, NT) + dot(tail, chosen, NT)).astype(BF16)
    two_sum.back_row()
    one_sum.back_col()
    one_sum.back_row()
    two_sum.end()
    one_sum.end()

    others(c, n_col, lambda peer: coarse_copy(c, peer, peer).wait_send())
    for x, y in BESIDE:
        @pl.when(beside(x, y))
        def _():
            halo_copy(x, y).wait_send()


def body(features, preact, coarse_grad, kernel_one, kernel_two, neighbours, send_list,
         parent_slot, child_pos):
    channels, sites = features.shape
    wide, parents = coarse_grad.shape
    offsets = neighbours.shape[0]
    width = send_list.shape[0]
    padded = -(-width // 128) * 128
    n_col, n_row = lax.axis_size("col"), lax.axis_size("row")
    held = parents // n_col
    lines = -(-held // 16) * 16
    pairs = (offsets + 1) // 2
    one_rows, two_rows = pairs * channels, 8 * channels
    one_share, two_share = (-(-rows // (n_col * n_row * 16)) * 16 for rows in (one_rows, two_rows))
    shape = jax.ShapeDtypeStruct
    coarse = jnp.pad(coarse_grad.T.reshape(n_col, held, wide), ((0, 0), (0, lines - held), (0, 0)))
    two = kernel_two.transpose(0, 2, 1).reshape(8 * channels, wide)
    one = kernel_one.reshape(offsets * channels, channels)
    send = jnp.pad(send_list, (0, padded - width), constant_values=-1)[None, :]
    args = (coarse, parent_slot[None, :], child_pos[None, :], preact, features, two, one, neighbours,
            send)
    vmem = pl.BlockSpec(memory_space=pltpu.VMEM)
    sum_scratch, sum_sems = [], []
    for share in (one_share, two_share):
        sum_scratch += [
            pltpu.VMEM((n_row * n_col * share, wide), BF16),
            pltpu.VMEM((n_row, n_col * share, wide), BF16),
            pltpu.VMEM((n_col * share, wide), BF16),
            pltpu.VMEM((n_col, share, wide), BF16),
            pltpu.VMEM((share, wide), BF16),
        ]
        sum_sems += [pltpu.SemaphoreType.DMA((2, n)) for n in (n_row, n_col, n_col, n_row)]
    feat_grad, one_sum, two_sum = pl.pallas_call(
        functools.partial(kernel, (n_col, n_row, width, held, one_share, two_share)),
        out_shape=(shape((channels, sites), BF16), shape((n_row, n_col, one_share, wide), BF16),
                   shape((n_row, n_col, two_share, wide), BF16)),
        in_specs=[vmem] * len(args),
        out_specs=(vmem, vmem, vmem),
        scratch_shapes=[
            pltpu.VMEM((n_col, lines, wide), BF16),
            pltpu.VMEM((channels, sites), BF16),
            pltpu.VMEM((channels, padded), BF16),
            pltpu.VMEM((9, channels, padded), BF16),
            pltpu.VMEM((2 * pairs * channels, sites), BF16),
            pltpu.VMEM((2 * pairs * channels, padded), BF16),
            pltpu.VMEM((2, 2 * channels, sites), BF16),
            pltpu.VMEM((sites, sites), BF16),
            pltpu.VMEM((offsets, sites // 8, sites // 8), BF16),
            *sum_scratch,
            *sum_sems,
            pltpu.SemaphoreType.DMA((2, n_col)),
            pltpu.SemaphoreType.DMA((2, 9)),
        ],
        compiler_params=pltpu.CompilerParams(
            collective_id=0, has_side_effects=True, vmem_limit_bytes=48 * 1024 * 1024),
    )(*args)
    scale = float(sites * n_col * n_row) ** (-0.5)
    one_sum = one_sum.reshape(-1, wide)[:one_rows].reshape(pairs, channels, wide)
    one_sum = jnp.concatenate([one_sum[:, :, :channels], one_sum[:, :, channels:]])[:offsets]
    two_sum = two_sum.reshape(-1, wide)[:two_rows].reshape(8, channels, wide).transpose(0, 2, 1)
    return feat_grad, one_sum.astype(F32) * scale, two_sum.astype(F32) * scale


def solution(mesh):
    both = ("col", "row")
    placed = (P(None, both), P(None, both), P(None, both), P(), P(), P(None, both), P(both),
              P(both), P(both))
    return jax.shard_map(body, mesh=mesh, in_specs=placed, out_specs=(P(None, both), P(), P()),
                         check_vma=False)
```

```python
import functools

import jax
import jax.numpy as jnp
from jax import lax
from jax.experimental import pallas as pl
from jax.experimental.pallas import tpu as pltpu
from jax.sharding import PartitionSpec as P

F32 = jnp.float32
BF16 = jnp.bfloat16
NN = (((1,), (0,)), ((), ()))
NT = (((1,), (1,)), ((), ()))
TN = (((0,), (0,)), ((), ()))
MESH = pl.DeviceIdType.MESH
BESIDE = [(x, y) for x in (-1, 0, 1) for y in (-1, 0, 1) if (x, y) != (0, 0)]


def pick(index_row, rows):
    n = index_row.shape[1]
    spot = lax.broadcasted_iota(jnp.int32, (rows, n), 0)
    return jnp.where(spot == index_row, 1.0, 0.0).astype(BF16)


def dot(a, b, dims=NN):
    return lax.dot_general(a, b, dims, preferred_element_type=F32)


def remote(src, dst, send_sem, recv_sem, col, row):
    return pltpu.make_async_remote_copy(
        src_ref=src, dst_ref=dst, send_sem=send_sem, recv_sem=recv_sem,
        device_id=(col, row), device_id_type=MESH)


def others(me, count, step):
    for j in range(1, count):
        step(lax.rem(me + j, count))


def landed(pieces, sem):
    pltpu.make_async_copy(pieces, pieces, sem).wait()


class Sum:
    def __init__(self, place, share, part, row_in, mid, col_in, fin, out, row_sems, col_sems,
                 back_col_sems, back_row_sems):
        self.c, self.r, self.n_col, self.n_row = place
        self.share, self.band = share, share * self.n_col
        self.part, self.row_in, self.mid, self.col_in = part, row_in, mid, col_in
        self.fin, self.out = fin, out
        self.sems = (row_sems, col_sems, back_col_sems, back_row_sems)

    def rows(self, step):
        others(self.r, self.n_row, step)

    def cols(self, step):
        others(self.c, self.n_col, step)

    def row_copy(self, src, dst, to):
        cut = pl.ds(pl.multiple_of(dst * self.band, self.band), self.band)
        return remote(self.part.at[cut], self.row_in.at[src], self.sems[0].at[0],
                      self.sems[0].at[1], self.c, to)

    def col_copy(self, src, dst, to):
        cut = pl.ds(pl.multiple_of(dst * self.share, self.share), self.share)
        return remote(self.mid.at[cut], self.col_in.at[src], self.sems[1].at[0],
                      self.sems[1].at[1], to, self.r)

    def back_col_copy(self, src, dst, to):
        return remote(self.fin, self.out.at[self.r, src], self.sems[2].at[0],
                      self.sems[2].at[1], to, self.r)

    def back_row_copy(self, src, dst, to):
        return remote(self.out.at[src], self.out.at[src], self.sems[3].at[0],
                      self.sems[3].at[1], self.c, to)

    def start(self):
        self.rows(lambda peer: self.row_copy(self.r, peer, peer).start())
        self.row_in[pl.ds(self.r, 1)] = self.part[
            pl.ds(pl.multiple_of(self.r * self.band, self.band), self.band), :][None]

    def along_col(self):
        landed(self.row_in.at[pl.ds(0, self.n_row - 1)], self.sems[0].at[1])
        total = self.row_in[0].astype(F32)
        for i in range(1, self.n_row):
            total = total + self.row_in[i].astype(F32)
        self.mid[...] = total.astype(BF16)
        self.cols(lambda peer: self.col_copy(self.c, peer, peer).start())
        self.col_in[pl.ds(self.c, 1)] = self.mid[
            pl.ds(pl.multiple_of(self.c * self.share, self.share), self.share), :][None]

    def back_col(self):
        landed(self.col_in.at[pl.ds(0, self.n_col - 1)], self.sems[1].at[1])
        total = self.col_in[0].astype(F32)
        for i in range(1, self.n_col):
            total = total + self.col_in[i].astype(F32)
        self.fin[...] = total.astype(BF16)
        self.cols(lambda peer: self.back_col_copy(self.c, peer, peer).start())
        self.out[pl.ds(self.r, 1), pl.ds(self.c, 1)] = self.fin[...][None, None]

    def back_row(self):
        landed(self.out.at[0, pl.ds(0, self.n_col - 1)], self.sems[2].at[1])
        self.rows(lambda peer: self.back_row_copy(self.r, peer, peer).start())

    def end(self):
        landed(self.out.at[pl.ds(0, self.n_row - 1)], self.sems[3].at[1])
        landed(self.row_in.at[pl.ds(0, self.n_row - 1)], self.sems[0].at[0])
        landed(self.col_in.at[pl.ds(0, self.n_col - 1)], self.sems[1].at[0])
        landed(self.col_in.at[pl.ds(0, self.n_col - 1)], self.sems[2].at[0])
        landed(self.out.at[pl.ds(0, self.n_row - 1)], self.sems[3].at[0])


def offset_of(x, y, z):
    return (x + 1) * 9 + (y + 1) * 3 + z + 1


def bits(child):
    return child // 4, child // 2 % 2, child % 2


def kernel(sizes, coarse_ref, *refs):
    count = 8
    load_sems = refs[-count - 1]
    held = refs[-count:]
    loads = [pltpu.make_async_copy(refs[i], held[i], load_sems.at[i]) for i in range(count)]
    for load in loads:
        load.start()
    work(sizes, loads, load_sems.at[count], coarse_ref, *held, *refs[count:-count - 1])


def work(sizes, loads, own_sem, coarse_ref, slot_ref, child_ref, send_ref, nb_ref, feat_ref, preact_ref,
         two_ref, one_ref, feat_out_ref, one_sum_ref, two_sum_ref,
         owners, grad, offer, halo, ng, ngr, feat_two, sort, moves, *rest):
    n_col, n_row, width, held, one_share, two_share = sizes
    channels, sites = feat_ref.shape
    parents = sites // 8
    offsets = nb_ref.shape[0]
    pairs = (offsets + 1) // 2
    padded = send_ref.shape[1]
    c, r = lax.axis_index("col"), lax.axis_index("row")
    place = (c, r, n_col, n_row)
    one_sum = Sum(place, one_share, *rest[0:5], one_sum_ref, *rest[10:14])
    two_sum = Sum(place, two_share, *rest[5:10], two_sum_ref, *rest[14:18])
    coarse_sems, halo_sems = rest[18:]

    def beside(x, y):
        return ((c + x >= 0) & (c + x < n_col) & (r + y >= 0) & (r + y < n_row))

    barrier = pltpu.get_barrier_semaphore()

    def greet(col, row):
        pl.semaphore_signal(barrier, inc=1, device_id=(col, row), device_id_type=MESH)

    others(c, n_col, lambda peer: greet(peer, r))
    others(r, n_row, lambda peer: greet(c, peer))
    count = n_col - 1 + n_row - 1
    for x, y in BESIDE:
        if x != 0 and y != 0:
            there = beside(x, y)

            @pl.when(there)
            def _():
                greet(c + x, r + y)

            count = count + jnp.where(there, 1, 0)
    pl.semaphore_wait(barrier, count)

    def coarse_copy(src_col, dst_col, to):
        return remote(coarse_ref.at[dst_col], owners.at[src_col], coarse_sems.at[0],
                      coarse_sems.at[1], to, r)

    others(c, n_col, lambda peer: coarse_copy(c, peer, peer).start())
    own = pltpu.make_async_copy(coarse_ref.at[c], owners.at[c], own_sem)
    own.start()
    for x, y in BESIDE:
        @pl.when(jnp.logical_not(beside(x, y)))
        def _():
            halo[(x + 1) * 3 + y + 1] = jnp.zeros(halo.shape[1:], BF16)

    for load in loads[:5]:
        load.wait()

    nb = nb_ref[...]
    high = nb // 64
    low = (nb - high * 64).astype(F32).astype(BF16)
    high = high.astype(F32).astype(BF16)

    pad = jnp.zeros((-offsets % 16, sites), BF16)
    table = jnp.concatenate([high, pad, low, pad, feat_ref[...]], axis=0)
    low_at = offsets + pad.shape[0]

    def entries(onehot, dims=NN):
        got = dot(table, onehot, dims)
        entry = got[:offsets] * 64.0 + got[low_at:low_at + offsets]
        return entry.astype(jnp.int32), got[2 * low_at:].astype(BF16)

    slot = slot_ref[...]
    child = child_ref[...]
    kinds = lax.broadcasted_iota(jnp.int32, (128, sites), 0)
    first = jnp.where((kinds == child) & (slot == 0), 1.0, 0.0).astype(BF16)
    first_nb, _ = entries(first, NT)
    slot_mark = jnp.broadcast_to((slot + 1).astype(F32), (16, sites)).astype(BF16)
    kind = jnp.zeros((16, 128), F32)
    for weight, o in ((4.0, offset_of(-1, 0, 0)), (2.0, offset_of(0, -1, 0)),
                      (1.0, offset_of(0, 0, -1))):
        mark = dot(slot_mark, pick(first_nb[o:o + 1, :], sites))
        kind = kind + jnp.where(mark == 1.0, weight, 0.0)
    corner = dot(kind.astype(BF16), pick(child, 128))[0:1, :].astype(jnp.int32)

    sort[...] = pick(corner * parents + slot, sites)
    sorted_nb, feat = entries(sort[...], NT)
    feat_two[0, pl.ds(0, channels), :] = feat
    feat_two[0, pl.ds(channels, channels), :] = jnp.zeros((channels, sites), BF16)
    feat_two[1, pl.ds(0, channels), :] = jnp.zeros((channels, sites), BF16)
    feat_two[1, pl.ds(channels, channels), :] = feat
    chosen_slot = pick(slot, parents)
    def ahead(o):
        x, y, z = o // 9 - 1, o // 3 % 3 - 1, o % 3 - 1
        at = ((x > 0) * 4 + (y > 0) * 2 + (z > 0)) * parents
        return sorted_nb[o:o + 1, at:at + parents]

    for o in range(offsets // 2):
        mirror = offsets - 1 - o
        both = jnp.concatenate([ahead(o), ahead(mirror)], axis=1)
        found = dot(chosen_slot, pick(both, sites)).astype(BF16)
        moves[o] = found[:, :parents]
        moves[mirror] = found[:, parents:]
    chosen = pick(send_ref[...], sites)
    rim, rim_feat = entries(chosen)
    blank = jnp.zeros(rim_feat.shape, BF16)

    loads[5].wait()
    pre = preact_ref[...].astype(F32)
    gate = jax.nn.sigmoid(pre)
    act = (pre * gate).astype(BF16).astype(F32)
    lines = owners.shape[1]
    chosen_parent = pick(slot // held * lines + slot % held, n_col * lines)
    ng[pl.ds(offsets * channels, channels), :] = jnp.zeros((channels, sites), BF16)
    ngr[pl.ds(offsets * channels, channels), :] = jnp.zeros((channels, padded), BF16)
    own.wait()
    landed(owners.at[pl.ds(0, n_col - 1)], coarse_sems.at[1])
    all_owned = owners[...].reshape(n_col * lines, owners.shape[2])
    parent = dot(all_owned.astype(F32).T.astype(BF16), chosen_parent).astype(BF16)
    loads[6].wait()
    products = dot(two_ref[...], parent)
    act_grad = products[:channels]
    for k in range(1, 8):
        here = jnp.broadcast_to(child == k, (channels, sites))
        act_grad = jnp.where(here, products[k * channels:(k + 1) * channels], act_grad)
    grad[...] = (act_grad * gate * (1.0 + pre * (1.0 - gate))).astype(BF16)
    offer[...] = dot(grad[...], chosen).astype(BF16)

    def halo_copy(x, y):
        b = (x + 1) * 3 + y + 1
        return remote(offer, halo.at[8 - b], halo_sems.at[0, b], halo_sems.at[1, 8 - b],
                      c + x, r + y)

    for x, y in BESIDE:
        @pl.when(beside(x, y))
        def _():
            halo_copy(x, y).start()

    two_rows = 8 * channels
    masked = jnp.concatenate([
        jnp.where(jnp.broadcast_to(child == k, (channels, sites)), act, 0.0).astype(BF16)
        for k in range(8)], axis=0)
    two_sum.part[pl.ds(0, two_rows), :] = dot(masked, parent, NT).astype(BF16)
    base = pairs * channels
    for piece, used in ((two_sum.part, two_rows), (one_sum.part, base)):
        spare = piece.shape[0] - used
        if spare > 0:
            piece[pl.ds(used, spare), :] = jnp.zeros((spare, piece.shape[1]), BF16)
    two_sum.start()

    near = dot(grad[...], sort[...], NT).astype(BF16)
    blocks = [near[:, k * parents:(k + 1) * parents] for k in range(8)]
    found = {((0, 0, 0), k): blocks[k] for k in range(8)}
    for o in range(offsets):
        if o != offsets // 2:
            step = (o // 9 - 1, o // 3 % 3 - 1, o % 3 - 1)
            ends = [k for k in range(8)
                    if all(s == 0 or b == (s < 0) for s, b in zip(step, bits(k)))]
            moved = dot(jnp.concatenate([blocks[k] for k in ends], axis=0), moves[o]).astype(BF16)
            for i, k in enumerate(ends):
                found[step, k] = moved[i * channels:(i + 1) * channels, :]
    for o in range(offsets):
        move = (1 - o // 9, 1 - o // 3 % 3, 1 - o % 3)
        for k in range(8):
            to = [b + m for b, m in zip(bits(k), move)]
            end = to[0] % 2 * 4 + to[1] % 2 * 2 + to[2] % 2
            ng[pl.ds(o * channels, channels), pl.ds(k * parents, parents)] = (
                found[tuple(t // 2 for t in to), end])
    two_sum.along_col()
    loads[7].wait()
    spread = dot(one_ref[...], ng[pl.ds(0, offsets * channels), :], TN)

    def split(values):
        head = values.astype(BF16)
        return jnp.concatenate([head, (values - head.astype(F32)).astype(BF16)], axis=0)

    def joined(halves):
        return halves[:channels] + halves[channels:]

    feat_grad = joined(dot(split(spread), sort[...]))
    one_grad = dot(ng[pl.ds(0, base), :], feat_two[0], NT) + dot(
        ng[pl.ds(base, base), :], feat_two[1], NT)

    for x, y in BESIDE:
        @pl.when(beside(x, y))
        def _():
            halo_copy(-x, -y).wait_recv()
    for o in range(offsets):
        mirror = offsets - 1 - o
        ex, ey = mirror // 9 - 1, mirror // 3 % 3 - 1
        total = jnp.zeros((channels, padded), F32)
        for gx, gy in sorted({(ex, 0), (0, ey), (ex, ey)} - {(0, 0)}):
            b = (gx + 1) * 3 + gy + 1
            index = rim[mirror:mirror + 1, :] - (sites + b * width)
            total = total + dot(halo[b], pick(index, padded))
        ngr[pl.ds(o * channels, channels), :] = total.astype(BF16)
    one_grad = one_grad + dot(
        ngr[pl.ds(0, base), :], jnp.concatenate([rim_feat, blank], axis=0), NT) + dot(
        ngr[pl.ds(base, base), :], jnp.concatenate([blank, rim_feat], axis=0), NT)
    one_sum.part[pl.ds(0, base), :] = one_grad.astype(BF16)
    one_sum.start()
    two_sum.back_col()
    one_sum.along_col()
    extra = dot(one_ref[...], ngr[pl.ds(0, offsets * channels), :], TN)
    feat_out_ref[...] = (feat_grad + joined(dot(split(extra), chosen, NT))).astype(BF16)
    two_sum.back_row()
    one_sum.back_col()
    one_sum.back_row()
    two_sum.end()
    one_sum.end()

    landed(owners.at[pl.ds(0, n_col - 1)], coarse_sems.at[0])
    for x, y in BESIDE:
        @pl.when(beside(x, y))
        def _():
            halo_copy(x, y).wait_send()


def finish(scale, feat_in, one_in, two_in, feat_out, one_out, two_out, feat_ref, one_ref, two_ref,
           one, two, sems):
    loads = [pltpu.make_async_copy(src, dst, sems.at[3 + i]) for i, (src, dst) in enumerate(
        ((feat_in, feat_ref), (one_in, one_ref), (two_in, two_ref)))]
    for load in loads:
        load.start()
    offsets, channels, _ = one.shape
    pairs = (offsets + 1) // 2
    sent = [pltpu.make_async_copy(src, dst, sems.at[i])
            for i, (src, dst) in enumerate(((feat_ref, feat_out), (one, one_out), (two, two_out)))]
    loads[0].wait()
    sent[0].start()
    loads[1].wait()
    sums = one_ref[pl.ds(0, pairs * channels), :].astype(F32) * scale
    sums = sums.reshape(pairs, channels, 2 * channels)
    one[pl.ds(0, pairs)] = sums[:, :, :channels]
    one[pl.ds(pairs, offsets - pairs)] = sums[:offsets - pairs, :, channels:]
    sent[1].start()
    loads[2].wait()
    two[...] = two_ref[pl.ds(0, two.shape[0]), :].astype(F32) * scale
    sent[2].start()
    for copy in sent:
        copy.wait()


def body(features, preact, coarse_grad, kernel_one, kernel_two, neighbours, send_list,
         parent_slot, child_pos):
    channels, sites = features.shape
    wide, parents = coarse_grad.shape
    offsets = neighbours.shape[0]
    width = send_list.shape[0]
    padded = -(-width // 128) * 128
    n_col, n_row = lax.axis_size("col"), lax.axis_size("row")
    held = parents // n_col
    lines = -(-held // 16) * 16
    pairs = (offsets + 1) // 2
    one_rows, two_rows = pairs * channels, 8 * channels
    one_share, two_share = (-(-rows // (n_col * n_row * 16)) * 16 for rows in (one_rows, two_rows))
    shape = jax.ShapeDtypeStruct
    coarse = jnp.pad(coarse_grad.T.reshape(n_col, held, wide), ((0, 0), (0, lines - held), (0, 0)))
    two = kernel_two.transpose(0, 2, 1).reshape(8 * channels, wide)
    one = kernel_one.reshape(offsets * channels, channels)
    send = jnp.pad(send_list, (0, padded - width), constant_values=-1)[None, :]
    held_args = (parent_slot[None, :], child_pos[None, :], send, neighbours, features, preact, two, one)
    anywhere = pl.BlockSpec(memory_space=pl.ANY)
    vmem = pl.BlockSpec(memory_space=pltpu.VMEM)
    sum_scratch, sum_sems = [], []
    for share in (one_share, two_share):
        sum_scratch += [
            pltpu.VMEM((n_row * n_col * share, wide), BF16),
            pltpu.VMEM((n_row, n_col * share, wide), BF16),
            pltpu.VMEM((n_col * share, wide), BF16),
            pltpu.VMEM((n_col, share, wide), BF16),
            pltpu.VMEM((share, wide), BF16),
        ]
        sum_sems += [pltpu.SemaphoreType.DMA((2,))] * 4
    feat_grad, one_sum, two_sum = pl.pallas_call(
        functools.partial(kernel, (n_col, n_row, width, held, one_share, two_share)),
        out_shape=(shape((channels, sites), BF16), shape((n_row, n_col, one_share, wide), BF16),
                   shape((n_row, n_col, two_share, wide), BF16)),
        in_specs=[anywhere] * (1 + len(held_args)),
        out_specs=(vmem, vmem, vmem),
        scratch_shapes=[
            pltpu.VMEM((n_col, lines, wide), BF16),
            pltpu.VMEM((channels, sites), BF16),
            pltpu.VMEM((channels, padded), BF16),
            pltpu.VMEM((9, channels, padded), BF16),
            pltpu.VMEM((2 * pairs * channels, sites), BF16),
            pltpu.VMEM((2 * pairs * channels, padded), BF16),
            pltpu.VMEM((2, 2 * channels, sites), BF16),
            pltpu.VMEM((sites, sites), BF16),
            pltpu.VMEM((offsets, sites // 8, sites // 8), BF16),
            *sum_scratch,
            *sum_sems,
            pltpu.SemaphoreType.DMA((2,)),
            pltpu.SemaphoreType.DMA((2, 9)),
            pltpu.SemaphoreType.DMA((1 + len(held_args),)),
            *[pltpu.VMEM(x.shape, x.dtype) for x in held_args],
        ],
        compiler_params=pltpu.CompilerParams(
            collective_id=0, has_side_effects=True, vmem_limit_bytes=56 * 1024 * 1024),
    )(coarse, *held_args)
    scale = float(sites * n_col * n_row) ** (-0.5)
    sums = feat_grad, one_sum.reshape(-1, wide), two_sum.reshape(-1, wide)
    outs = (feat_grad.shape, BF16), ((offsets, channels, channels), F32), ((two_rows, wide), F32)
    feat_grad, one_sum, two_sum = pl.pallas_call(
        functools.partial(finish, scale),
        out_shape=tuple(shape(*out) for out in outs),
        in_specs=[anywhere] * 3,
        out_specs=(anywhere,) * 3,
        scratch_shapes=[
            *[pltpu.VMEM(x.shape, BF16) for x in sums],
            pltpu.VMEM(*outs[1]), pltpu.VMEM(*outs[2]), pltpu.SemaphoreType.DMA((6,)),
        ],
        compiler_params=pltpu.CompilerParams(vmem_limit_bytes=56 * 1024 * 1024),
    )(*sums)
    return feat_grad, one_sum, two_sum.reshape(8, channels, wide).transpose(0, 2, 1)


def solution(mesh):
    both = ("col", "row")
    placed = (P(None, both), P(None, both), P(None, both), P(), P(), P(None, both), P(both),
              P(both), P(both))
    return jax.shard_map(body, mesh=mesh, in_specs=placed, out_specs=(P(None, both), P(), P()),
                         check_vma=False)
```
